32 devices in a mesh: gx: 8 (over z, y), gy: 4 (over x, core).
Axes of the slice: x: 2, y: 2, z: 4, core: 2. Of those that a mesh axis runs over, the one named last changes fastest.
Arguments:
- layer_input: bfloat16 [128, 128, 32, 512], P('gx', 'gy'), may hold values from -6 to 6
- cotangent: bfloat16 [128, 128, 32, 512], P('gx', 'gy'), may hold values from -6 to 6
- spectral_weight: bfloat16 [32, 64, 32, 1024], P('gy', 'gx'), may hold values from -12 to 12
- bypass_weight: bfloat16 [32, 32], replicated, may hold values from -1 to 1
- channel_bias: float32 [32], replicated, may hold values from -4 to 4
- hash_key: int32 [2], replicated, may hold values from 0 to 1073741823
Outputs:
- grad_input: bfloat16 [128, 128, 32, 512], P('gx', 'gy')
- grad_spectral: float32 [32, 64, 32, 1024], P('gy', 'gx')
- grad_bypass: float32 [32, 32], replicated
- grad_bias: float32 [32], replicated
The draws below stay inside these ranges and needn't reach their ends.
All inputs are finite; a program needn't handle non-finite values.
Results may differ from the reference program's by a relative error of at most 0.011.
Values sent between devices are 32-bit elements; how exact they have to be, the bound alone decides.
A program may use at most 192 MiB of HBM per device.

```python
import math
import jax
import jax.numpy as jnp
from jax import lax

LX = 128
LY = 128
LZ = 64
LT = 8
C = 32
KX = 32
KY = 32
KZ = 16
KT = 4
LZT = 512
KZT = 64
CC = 1024


def level_of(rng, extent, cuts, smallest, high):
    loudness = 1.0
    for axis_at, shards_of in cuts:
        draws = jax.random.uniform(jax.random.fold_in(jax.random.fold_in(rng, 6), axis_at), (shards_of,), jnp.float32, smallest / len(cuts), high / len(cuts))
        loudness = loudness * jnp.repeat(jnp.exp(draws), extent[axis_at] // shards_of).reshape((-1,) + (1,) * (len(extent) - 1 - axis_at))
    return loudness


def gaussian(stream_key, shape, width, bound, pieces=(), held_as=jnp.bfloat16):
    level = level_of(stream_key, shape, pieces, -0.22, 0.18) if pieces else 1.0
    values = jax.random.normal(stream_key, shape, jnp.float32) * width * level
    return jnp.minimum(jnp.maximum(values, -bound), bound).astype(held_as)


def setup_inputs(seed: int = 0) -> dict:
    seeds = jax.random.split(jax.random.key(seed), 7)
    return {
        "layer_input": gaussian(seeds[0], (LX, LY, C, LZT), 1.0, 6.0, ((0, 8), (1, 4))),
        "cotangent": gaussian(seeds[1], (LX, LY, C, LZT), 1.0, 6.0, ((0, 8), (1, 4))),
        "spectral_weight": gaussian(seeds[2], (KY, KZT, KX, CC), 2.0, 12.0, ((0, 4), (1, 8))),
        "bypass_weight": gaussian(seeds[3], (C, C), C ** -0.5, 1.0),
        "channel_bias": gaussian(seeds[4], (C,), 1.0, 4.0, (), jnp.float32),
        "hash_key": jax.random.randint(seeds[5], (2,), 0, 1073741824).astype(jnp.int32),
    }


keep_level = 6554
keep_scale = 1.0 / 0.9
gelu_cubic = 0.044715
mixer_one = -1640531535
mixer_two = -2048144789
mixer_three = -1028477387

def hartley_table(kept, length):
    wanted = jnp.arange(kept, dtype=jnp.int32)
    frequency = jnp.where(wanted < kept // 2, wanted, wanted + (length - kept))
    positions = jnp.arange(length, dtype=jnp.int32)
    residue = frequency[:, None] * positions[None, :] % length
    radians = residue.astype(jnp.float32) * (2.0 * math.pi / length)
    return (jnp.cos(radians) + jnp.sin(radians)) / math.sqrt(length)

def depth_table():
    depth_part = hartley_table(KZ, LZ)
    time_part = hartley_table(KT, LT)
    joined = depth_part[:, None, :, None] * time_part[None, :, None, :]
    return joined.reshape(KZ * KT, LZ * LT)

def scramble(hashed):
    hashed = jnp.bitwise_xor(hashed, lax.shift_right_logical(hashed, jnp.int32(16)))
    hashed = hashed * jnp.int32(mixer_two)
    hashed = jnp.bitwise_xor(hashed, lax.shift_right_logical(hashed, jnp.int32(13)))
    hashed = hashed * jnp.int32(mixer_three)
    return jnp.bitwise_xor(hashed, lax.shift_right_logical(hashed, jnp.int32(16)))

def dropout_keep(cell_index, hash_key):
    hashed = cell_index * jnp.int32(mixer_one) + hash_key[0]
    hashed = scramble(hashed)
    hashed = scramble(jnp.bitwise_xor(hashed, hash_key[1]))
    return jnp.bitwise_and(hashed, jnp.int32(65535)) >= keep_level

def gelu_slope(preact):
    factor = math.sqrt(2.0 / math.pi)
    tanh_value = jnp.tanh(factor * (preact + gelu_cubic * preact * preact * preact))
    return 0.5 * (1.0 + tanh_value) + 0.5 * preact * (1.0 - tanh_value * tanh_value) * factor * (1.0 + 3.0 * gelu_cubic * preact * preact)

def reference(layer_input, cotangent, spectral_weight, bypass_weight, channel_bias, hash_key):
    highest = lax.Precision.HIGHEST
    across_table = hartley_table(KX, LX)
    down_table = hartley_table(KY, LY)
    depth_full = depth_table()
    depth_low = depth_full.T.astype(jnp.bfloat16)
    weight_modes = spectral_weight.astype(jnp.float32).reshape(KY, KZT, KX, C, C)
    bypass_wide = bypass_weight.astype(jnp.float32)

    def forward_modes(source):

        def one_plane(plane):
            depth_part = jnp.dot(plane.reshape(LY * C, LZT), depth_low, preferred_element_type=jnp.float32)
            return jnp.einsum('ky,ycm->kcm', down_table, depth_part.reshape(LY, C, KZT), precision=highest)
        planes = lax.map(one_plane, source)
        return jnp.einsum('jx,xkcm->jkcm', across_table, planes, precision=highest)

    def plane_cells(plane_modes):
        column_modes = jnp.einsum('ky,kcm->ycm', down_table, plane_modes, precision=highest)
        flattened = jnp.dot(column_modes.reshape(LY * C, KZT), depth_full, precision=highest, preferred_element_type=jnp.float32)
        return flattened.reshape(LY, C, LZT)
    column_ids = jnp.arange(LY, dtype=jnp.int32)
    channel_ids = jnp.arange(C, dtype=jnp.int32)
    depth_ids = jnp.arange(LZT, dtype=jnp.int32)
    plane_ids = jnp.arange(LX, dtype=jnp.int32)
    input_modes = forward_modes(layer_input)
    mixed_modes = jnp.einsum('jkcm,kmjcd->jkdm', input_modes, weight_modes, precision=highest)
    spread = jnp.einsum('jx,jkcm->xkcm', across_table, mixed_modes, precision=highest)

    def first_pass(plane_items):
        plane_modes, plane, cot_plane, plane_row = plane_items
        spectral = plane_cells(plane_modes)
        bypass = jnp.einsum('yct,cd->ydt', plane.astype(jnp.float32), bypass_wide, precision=highest)
        preact = spectral + bypass + channel_bias[None, :, None]
        cell_index = ((plane_row * LY + column_ids[:, None, None]) * C + channel_ids[None, :, None]) * LZT + depth_ids[None, None, :]
        keep_mask = dropout_keep(cell_index, hash_key)
        dpre = jnp.where(keep_mask, cot_plane.astype(jnp.float32) * gelu_slope(preact) * keep_scale, 0.0).astype(jnp.bfloat16)
        wide_dpre = dpre.astype(jnp.float32)
        weight_part = jnp.einsum('yct,ydt->cd', plane.astype(jnp.float32), wide_dpre, precision=highest)
        bias_part = lax.optimization_barrier(jnp.sum(wide_dpre, axis=(0, 2)))
        return (dpre, weight_part, bias_part)
    dpre, weight_parts, bias_parts = lax.map(first_pass, (spread, layer_input, cotangent, plane_ids))
    norm_scale = 1.0 / math.sqrt(LX * LY * LZT)
    grad_bypass = lax.optimization_barrier(jnp.sum(weight_parts, axis=0)) * norm_scale
    grad_bias = lax.optimization_barrier(jnp.sum(bias_parts, axis=0)) * norm_scale
    dpre_modes = forward_modes(dpre)
    grad_spectral = jnp.einsum('jkcm,jkdm->kmjcd', input_modes, dpre_modes, precision=highest).reshape(KY, KZT, KX, C * C)
    backward_modes = jnp.einsum('jkdm,kmjcd->jkcm', dpre_modes, weight_modes, precision=highest)
    spread_back = jnp.einsum('jx,jkcm->xkcm', across_table, backward_modes, precision=highest)

    def second_pass(plane_items):
        plane_modes, dpre_plane = plane_items
        local_part = jnp.einsum('ydt,cd->yct', dpre_plane.astype(jnp.float32), bypass_wide, precision=highest)
        return (plane_cells(plane_modes) + local_part).astype(jnp.bfloat16)
    grad_input = lax.map(second_pass, (spread_back, dpre))
    return (grad_input, grad_spectral, grad_bypass, grad_bias)
```

```python
import functools
import math

import jax
import jax.numpy as jnp
import ml_dtypes
import numpy as np
from jax import lax
from jax.experimental import pallas as pl
from jax.experimental.pallas import tpu as pltpu
from jax.sharding import PartitionSpec as P

LZ = 64
LT = 8
KZ = 16
KT = 4

keep_level = 6554
keep_scale = 1.0 / 0.9
gelu_cubic = 0.044715
mixer_one = -1640531535
mixer_two = -2048144789
mixer_three = -1028477387
low = jnp.bfloat16
wide = jnp.float32
VMEM_LIMIT = 56 * 1024 * 1024


def hartley_table(kept, length):
    wanted = np.arange(kept)
    frequency = np.where(wanted < kept // 2, wanted, wanted + (length - kept))
    residue = frequency[:, None] * np.arange(length)[None, :] % length
    radians = residue * (2.0 * math.pi / length)
    return (np.cos(radians) + np.sin(radians)) / math.sqrt(length)


def depth_table():
    depth_part = hartley_table(KZ, LZ)
    time_part = hartley_table(KT, LT)
    joined = depth_part[:, None, :, None] * time_part[None, :, None, :]
    return joined.reshape(KZ * KT, LZ * LT)


def low_constant(values):
    return jnp.asarray(np.asarray(values, np.float32).astype(ml_dtypes.bfloat16))


def low_pair(values):
    high = np.asarray(values, np.float32).astype(ml_dtypes.bfloat16)
    return jnp.asarray(high), low_constant(values - high.astype(np.float64))


def halves(values):
    high = values.astype(low)
    return high, (values - high.astype(wide)).astype(low)


def scramble(hashed):
    hashed = jnp.bitwise_xor(hashed, lax.shift_right_logical(hashed, jnp.int32(16)))
    hashed = hashed * jnp.int32(mixer_two)
    hashed = jnp.bitwise_xor(hashed, lax.shift_right_logical(hashed, jnp.int32(13)))
    hashed = hashed * jnp.int32(mixer_three)
    return jnp.bitwise_xor(hashed, lax.shift_right_logical(hashed, jnp.int32(16)))


def scaled_slope(preact):
    factor = math.sqrt(2.0 / math.pi)
    square = preact * preact
    tanh_value = jnp.tanh(preact * (square * (factor * gelu_cubic) + factor))
    inner = preact * (
        square * (0.5 * keep_scale * factor * 3.0 * gelu_cubic) + 0.5 * keep_scale * factor
    )
    return (1.0 + tanh_value) * (inner * (1.0 - tanh_value) + 0.5 * keep_scale)


def dot(a, b):
    return lax.dot_general(a, b, (((1,), (0,)), ((), ())), preferred_element_type=wide)


def dot_rows(a, b):
    return lax.dot_general(a, b, (((1,), (1,)), ((), ())), preferred_element_type=wide)


def dot_fine(a, b):
    return dot(a[0], b[0]) + (dot(a[1], b[0]) + dot(a[0], b[1]))


def forward_kernel(source_ref, depth_ref, down_ref, rest_ref, out_ref, swept, swept_rest):
    rows = source_ref.shape[0]
    modes = depth_ref.shape[0]
    lanes = out_ref.shape[3]
    for row in range(rows):
        window = slice(row * modes, (row + 1) * modes)
        swept[window, :], swept_rest[window, :] = halves(dot_rows(depth_ref[...], source_ref[row]))
    for part in range(out_ref.shape[0]):
        window = slice(part * lanes, (part + 1) * lanes)
        out_ref[part] = dot_fine(
            (swept[...], swept_rest[...]), (down_ref[:, window], rest_ref[:, window])
        ).reshape(rows, modes, lanes)


def forward_local(source, depth_low, down_wide, down_rest, parts):
    slab_rows, cells, depth_cells = source.shape
    modes = depth_low.shape[0]
    lanes = down_wide.shape[1] // parts
    step = min(4, slab_rows)
    return pl.pallas_call(
        forward_kernel,
        grid=(slab_rows // step,),
        in_specs=[
            pl.BlockSpec((step, cells, depth_cells), lambda i: (i, 0, 0)),
            pl.BlockSpec(depth_low.shape, lambda i: (0, 0)),
            pl.BlockSpec(down_wide.shape, lambda i: (0, 0)),
            pl.BlockSpec(down_rest.shape, lambda i: (0, 0)),
        ],
        out_specs=pl.BlockSpec((parts, step, modes, lanes), lambda i: (0, i, 0, 0)),
        out_shape=jax.ShapeDtypeStruct((parts, slab_rows, modes, lanes), wide),
        scratch_shapes=[pltpu.VMEM((step * modes, cells), low)] * 2,
        compiler_params=pltpu.CompilerParams(vmem_limit_bytes=VMEM_LIMIT),
        name="forward_local",
    )(source, depth_low, down_wide, down_rest)


def mix_kernel(
    planes_ref,
    weight_ref,
    across_ref,
    across_rest,
    back_ref,
    back_rest,
    pick_c,
    sum_d,
    modes_ref,
    out_ref,
    split,
    mixed,
):
    ky = pl.program_id(0)
    steps, _, channels = split.shape

    @pl.when(ky == 0)
    def _():
        modes = dot_fine((across_ref[...], across_rest[...]), halves(planes_ref[...]))
        modes_ref[...] = modes
        for part in range(steps):
            split[part] = modes[:, part * channels : (part + 1) * channels]

    high, rest = halves(split[ky])
    spread = dot(high, pick_c[...]) + dot(rest, pick_c[...])
    high, rest = halves(spread * weight_ref[0].astype(wide))
    mixed[ky] = dot(high, sum_d[...]) + dot(rest, sum_d[...])

    @pl.when(ky == steps - 1)
    def _():
        joined = jnp.concatenate([mixed[part] for part in range(steps)], axis=1)
        out_ref[...] = dot_fine((back_ref[...], back_rest[...]), halves(joined))


def mix_back_kernel(
    planes_ref,
    modes_ref,
    weight_ref,
    across_ref,
    back_ref,
    pick_c,
    pick_d,
    sum_c,
    grad_ref,
    out_ref,
    split_in,
    split,
    mixed,
):
    ky = pl.program_id(0)
    steps, _, channels = split.shape

    @pl.when(ky == 0)
    def _():
        modes = dot(across_ref[...], planes_ref[...].astype(low))
        for part in range(steps):
            window = slice(part * channels, (part + 1) * channels)
            split[part] = modes[:, window].astype(low)
            split_in[part] = modes_ref[:, window].astype(low)

    spread = dot(split[ky], pick_d[...])
    grad_ref[0] = dot(split_in[ky], pick_c[...]) * spread
    product = spread.astype(low) * weight_ref[0]
    mixed[ky] = dot(product, sum_c[...]).astype(low)

    @pl.when(ky == steps - 1)
    def _():
        joined = jnp.concatenate([mixed[part] for part in range(steps)], axis=1)
        out_ref[...] = dot(back_ref[...], joined)


def whole_spec(array):
    return pl.BlockSpec(array.shape, lambda i: (0,) * array.ndim)


def mix_modes(planes, weight, across, across_rest, back, back_rest, pick_c, sum_d):
    kept_rows, lanes = across.shape[0], planes.shape[1]
    steps, _, pairs = weight.shape
    channels = lanes // steps
    return pl.pallas_call(
        mix_kernel,
        grid=(steps,),
        in_specs=[
            whole_spec(planes),
            pl.BlockSpec((1, kept_rows, pairs), lambda i: (i, 0, 0)),
            whole_spec(across),
            whole_spec(across_rest),
            whole_spec(back),
            whole_spec(back_rest),
            whole_spec(pick_c),
            whole_spec(sum_d),
        ],
        out_specs=[
            pl.BlockSpec((kept_rows, lanes), lambda i: (0, 0)),
            pl.BlockSpec(planes.shape, lambda i: (0, 0)),
        ],
        out_shape=[
            jax.ShapeDtypeStruct((kept_rows, lanes), wide),
            jax.ShapeDtypeStruct(planes.shape, wide),
        ],
        scratch_shapes=[
            pltpu.VMEM((steps, kept_rows, channels), wide),
            pltpu.VMEM((steps, kept_rows, channels), wide),
        ],
        compiler_params=pltpu.CompilerParams(vmem_limit_bytes=VMEM_LIMIT),
        name="mix_modes",
    )(planes, weight, across, across_rest, back, back_rest, pick_c, sum_d)


def mix_back(planes, modes, weight, across, back, pick_c, pick_d, sum_c):
    kept_rows, lanes = across.shape[0], planes.shape[1]
    steps, _, pairs = weight.shape
    channels = lanes // steps
    return pl.pallas_call(
        mix_back_kernel,
        grid=(steps,),
        in_specs=[
            whole_spec(planes),
            whole_spec(modes),
            pl.BlockSpec((1, kept_rows, pairs), lambda i: (i, 0, 0)),
            whole_spec(across),
            whole_spec(back),
            whole_spec(pick_c),
            whole_spec(pick_d),
            whole_spec(sum_c),
        ],
        out_specs=[
            pl.BlockSpec((1, kept_rows, pairs), lambda i: (i, 0, 0)),
            pl.BlockSpec(planes.shape, lambda i: (0, 0)),
        ],
        out_shape=[
            jax.ShapeDtypeStruct((steps, kept_rows, pairs), wide),
            jax.ShapeDtypeStruct(planes.shape, wide),
        ],
        scratch_shapes=[
            pltpu.VMEM((steps, kept_rows, channels), low),
            pltpu.VMEM((steps, kept_rows, channels), low),
            pltpu.VMEM((steps, kept_rows, channels), low),
        ],
        compiler_params=pltpu.CompilerParams(vmem_limit_bytes=VMEM_LIMIT),
        name="mix_back",
    )(planes, modes, weight, across, back, pick_c, pick_d, sum_c)


def joined_parts(gathered_ref):
    parts, devices, rows, owned, lanes = gathered_ref.shape
    return jnp.concatenate(
        [
            jnp.concatenate(
                [gathered_ref[part, :, row].reshape(devices * owned, lanes) for row in range(rows)],
                axis=0,
            )
            for part in range(parts)
        ],
        axis=1,
    )


def column_modes(gathered_ref, up_ref, turned):
    rows, _, modes = turned.shape
    columns = dot(joined_parts(gathered_ref).astype(low), up_ref[...])
    for row in range(rows):
        turned[row] = columns[row * modes : (row + 1) * modes, :].T.astype(low)


def column_modes_fine(gathered_ref, up_ref, up_rest, turned):
    rows, _, stacked = turned.shape
    modes = stacked // 3
    columns = dot_fine(halves(joined_parts(gathered_ref)), (up_ref[...], up_rest[...]))
    for row in range(rows):
        high, rest = halves(columns[row * modes : (row + 1) * modes, :].T)
        turned[row] = jnp.concatenate([high, rest, high], axis=1)


def middle_kernel(
    channels,
    gathered_ref,
    source_ref,
    cotangent_ref,
    up_ref,
    up_rest,
    depth_ref,
    depth_low_ref,
    down_ref,
    bypass_ref,
    bias_ref,
    dpre_ref,
    modes_ref,
    weight_ref,
    sums_ref,
    turned,
    preact,
    swept,
):
    step = pl.program_id(0)
    rows, cells, depth_cells = source_ref.shape
    modes = depth_low_ref.shape[0]
    lanes = modes_ref.shape[3]
    block = bypass_ref.shape[0]
    columns = cells // channels

    @pl.when(step == 0)
    def _():
        weight_ref[...] = jnp.zeros_like(weight_ref)
        sums_ref[...] = jnp.zeros_like(sums_ref)

    column_modes_fine(gathered_ref, up_ref, up_rest, turned)
    for row in range(rows):
        for start in range(0, cells, block):
            window = slice(start, start + block)
            preact[window, :] = dot(turned[row, window, :], depth_ref[...]) + dot(
                bypass_ref[...], source_ref[row, window, :]
            )
        def one_column(column, carry):
            start = pl.multiple_of(column * channels, channels)
            window = pl.ds(start, channels)
            slope = scaled_slope(preact[window, :] + bias_ref[...])
            value = cotangent_ref[row, window, :].astype(wide) * slope
            dpre_ref[row, window, :] = value.astype(low)
            return carry

        lax.fori_loop(0, columns, one_column, 0)
        depth_sums = dot_rows(depth_low_ref[...], dpre_ref[row])
        sums_ref[...] += depth_sums[:8, :]
        swept[row * modes : (row + 1) * modes, :] = depth_sums.astype(low)
        total = weight_ref[...]
        for start in range(0, cells, block):
            window = slice(start, start + block)
            total += dot_rows(source_ref[row, window, :], dpre_ref[row, window, :])
        weight_ref[...] = total
    for part in range(modes_ref.shape[0]):
        modes_ref[part] = dot(
            swept[...], down_ref[:, part * lanes : (part + 1) * lanes]
        ).reshape(rows, modes, lanes)


def middle_pass(
    gathered, source, cotangent, up, up_rest, depth, depth_low, down, bypass, bias
):
    parts, devices, slab_rows, owned, lanes = gathered.shape
    modes = devices * owned
    _, cells, depth_cells = source.shape
    channels = bias.shape[0]
    block = bypass.shape[0]
    step = min(4, slab_rows)
    row_spec = pl.BlockSpec((step, cells, depth_cells), lambda i: (i, 0, 0))
    part_spec = pl.BlockSpec((parts, step, modes, lanes), lambda i: (0, i, 0, 0))
    return pl.pallas_call(
        functools.partial(middle_kernel, channels),
        grid=(slab_rows // step,),
        in_specs=[
            pl.BlockSpec((parts, devices, step, owned, lanes), lambda i: (0, 0, i, 0, 0)),
            row_spec,
            row_spec,
            whole_spec(up),
            whole_spec(up_rest),
            whole_spec(depth),
            whole_spec(depth_low),
            whole_spec(down),
            whole_spec(bypass),
            whole_spec(bias),
        ],
        out_specs=[
            row_spec,
            part_spec,
            pl.BlockSpec((block, block), lambda i: (0, 0)),
            pl.BlockSpec((8, cells), lambda i: (0, 0)),
        ],
        out_shape=[
            jax.ShapeDtypeStruct(source.shape, low),
            jax.ShapeDtypeStruct((parts, slab_rows, modes, lanes), wide),
            jax.ShapeDtypeStruct((block, block), wide),
            jax.ShapeDtypeStruct((8, cells), wide),
        ],
        scratch_shapes=[
            pltpu.VMEM((step, cells, 3 * modes), low),
            pltpu.VMEM((cells, depth_cells), wide),
            pltpu.VMEM((step * modes, cells), low),
        ],
        compiler_params=pltpu.CompilerParams(vmem_limit_bytes=VMEM_LIMIT),
        name="middle_pass",
    )(gathered, source, cotangent, up, up_rest, depth, depth_low, down, bypass, bias)


def last_kernel(gathered_ref, dpre_ref, up_ref, depth_ref, bypass_ref, out_ref, turned):
    rows, cells, _ = dpre_ref.shape
    block = bypass_ref.shape[0]
    column_modes(gathered_ref, up_ref, turned)
    for row in range(rows):
        for start in range(0, cells, block):
            window = slice(start, start + block)
            out_ref[row, window, :] = (
                dot(turned[row, window, :], depth_ref[...])
                + dot(bypass_ref[...], dpre_ref[row, window, :])
            ).astype(low)


def last_pass(gathered, dpre, up, depth, bypass):
    parts, devices, slab_rows, owned, lanes = gathered.shape
    modes = devices * owned
    _, cells, depth_cells = dpre.shape
    step = min(4, slab_rows)
    row_spec = pl.BlockSpec((step, cells, depth_cells), lambda i: (i, 0, 0))
    return pl.pallas_call(
        last_kernel,
        grid=(slab_rows // step,),
        in_specs=[
            pl.BlockSpec((parts, devices, step, owned, lanes), lambda i: (0, 0, i, 0, 0)),
            row_spec,
            whole_spec(up),
            whole_spec(depth),
            whole_spec(bypass),
        ],
        out_specs=row_spec,
        out_shape=jax.ShapeDtypeStruct(dpre.shape, low),
        scratch_shapes=[pltpu.VMEM((step, cells, modes), low)],
        compiler_params=pltpu.CompilerParams(vmem_limit_bytes=VMEM_LIMIT),
        name="last_pass",
    )(gathered, dpre, up, depth, bypass)


MESH = pl.DeviceIdType.MESH


def neighbours():
    row, column = lax.axis_index("gx"), lax.axis_index("gy")
    core, side = column % 2, column // 2
    return row, column, side * 2 + 1 - core, (1 - side) * 2 + core


def greet(row, column, mate, across):
    row_devices = lax.axis_size("gx")
    barrier = pltpu.get_barrier_semaphore()
    for target in (mate, across):
        pl.semaphore_signal(barrier, inc=1, device_id=(row, target), device_id_type=MESH)

    def signal_peer(offset, carry):
        pl.semaphore_signal(
            barrier,
            inc=1,
            device_id=(lax.rem(row + offset, row_devices), column),
            device_id_type=MESH,
        )
        return carry

    lax.fori_loop(1, row_devices, signal_peer, 0)
    pl.semaphore_wait(barrier, row_devices + 1)


def send(source, target, semaphores, at, device):
    return pltpu.make_async_remote_copy(
        src_ref=source,
        dst_ref=target,
        send_sem=semaphores.at[(0, *at)],
        recv_sem=semaphores.at[(1, *at)],
        device_id=device,
        device_id_type=MESH,
    )


def to_owner_steps(partial_ref, out_ref, mate_in, across_out, across_in, peer_out, sems):
    mate_sem, across_sem, peer_sem = sems
    _, slab_rows, _, _ = partial_ref.shape
    row, column, mate, across = neighbours()
    core, side = column % 2, column // 2
    row_devices, owned = peer_out.shape[0], peer_out.shape[2]
    chunks = mate_sem.shape[2]
    rows = slab_rows // chunks

    def window(chunk):
        return pl.ds(chunk * rows, rows)

    def mate_copy(chunk, half):
        return send(
            partial_ref.at[half * 2 + 1 - core, window(chunk)],
            mate_in.at[half, window(chunk)],
            mate_sem,
            (half, chunk),
            (row, mate),
        )

    def across_copy(chunk):
        return send(
            across_out.at[window(chunk)],
            across_in.at[window(chunk)],
            across_sem,
            (chunk,),
            (row, across),
        )

    def peer_copy(chunk, offset):
        peer = lax.rem(row + offset, row_devices)
        return send(
            peer_out.at[peer, window(chunk)],
            out_ref.at[row, window(chunk)],
            peer_sem,
            (chunk, offset - 1),
            (peer, column),
        )

    def start(chunk):
        for half in range(2):
            mate_copy(chunk, half).start()

    def pair_sum(chunk):
        for half in range(2):
            mate_copy(chunk, half).wait_recv()
        across_out[window(chunk)] = (
            partial_ref[across, window(chunk)] + mate_in[1 - side, window(chunk)]
        )
        across_copy(chunk).start()

    def side_sum(chunk):
        across_copy(chunk).wait_recv()
        total = (
            partial_ref[column, window(chunk)] + mate_in[side, window(chunk)]
        ) + across_in[window(chunk)]
        for peer in range(row_devices):
            peer_out[peer, window(chunk)] = total[:, peer * owned : (peer + 1) * owned, :]

        def start_peer(offset, carry):
            peer_copy(chunk, offset).start()
            return carry

        lax.fori_loop(1, row_devices, start_peer, 0)
        out_ref[row, window(chunk)] = peer_out[row, window(chunk)]

    def finish():
        for chunk in range(chunks):

            def wait_peer(offset, carry):
                copy = peer_copy(chunk, offset)
                copy.wait_recv()
                copy.wait_send()
                return carry

            lax.fori_loop(1, row_devices, wait_peer, 0)
            across_copy(chunk).wait_send()
            for half in range(2):
                mate_copy(chunk, half).wait_send()

    return chunks, start, pair_sum, side_sum, finish


def to_owner_kernel(partial_ref, out_ref, mate_in, across_out, across_in, peer_out, *sems):
    greet(*neighbours())
    chunks, start, pair_sum, side_sum, finish = to_owner_steps(
        partial_ref, out_ref, mate_in, across_out, across_in, peer_out, sems
    )
    for chunk in range(chunks):
        start(chunk)
    for chunk in range(chunks):
        pair_sum(chunk)
    for chunk in range(chunks):
        side_sum(chunk)
    finish()


def masking_kernel(
    all_columns,
    channels,
    key_ref,
    partial_ref,
    cotangent_ref,
    out_ref,
    masked_ref,
    mate_in,
    across_out,
    across_in,
    peer_out,
    held,
    made,
    offsets,
    in_sem,
    out_sem,
    *sems,
):
    slab_rows, cells, depth_cells = cotangent_ref.shape
    columns = cells // channels

    def fetch(row):
        return pltpu.make_async_copy(
            cotangent_ref.at[row], held.at[row % 2], in_sem.at[row % 2]
        )

    def put(row):
        return pltpu.make_async_copy(made.at[row % 2], masked_ref.at[row], out_sem.at[row % 2])

    fetch(0).start()
    offsets[...] = (
        lax.broadcasted_iota(jnp.int32, offsets.shape, 0) * depth_cells
        + lax.broadcasted_iota(jnp.int32, offsets.shape, 1)
    ) * jnp.int32(mixer_one)
    greet(*neighbours())
    chunks, start, pair_sum, side_sum, finish = to_owner_steps(
        partial_ref, out_ref, mate_in, across_out, across_in, peer_out, sems
    )
    for chunk in range(chunks):
        start(chunk)
    plan = {row: [] for row in range(slab_rows)}
    for chunk in range(chunks):
        plan[min(chunk, slab_rows - 1)].append((pair_sum, chunk))
    for chunk in range(chunks):
        plan[min(slab_rows - 1, (chunk + 1) * slab_rows // chunks)].append((side_sum, chunk))
    row_base = lax.axis_index("gx") * slab_rows
    column_base = lax.axis_index("gy") * columns
    stride = (channels * depth_cells * mixer_one + 2**31) % 2**32 - 2**31
    for row in range(slab_rows):
        if row + 1 < slab_rows:
            fetch(row + 1).start()
        fetch(row).wait()
        if row >= 2:
            put(row - 2).wait()
        first = ((row_base + row) * all_columns + column_base) * jnp.int32(stride) + key_ref[0]

        def one_column(column, carry):
            window = pl.ds(pl.multiple_of(column * channels, channels), channels)
            hashed = scramble(offsets[...] + (first + column * jnp.int32(stride)))
            hashed = scramble(jnp.bitwise_xor(hashed, key_ref[1]))
            keep = jnp.bitwise_and(hashed, jnp.int32(65535)) >= keep_level
            made[row % 2, window, :] = jnp.where(
                keep, held[row % 2, window, :].astype(wide), 0.0
            ).astype(low)
            return carry

        lax.fori_loop(0, columns, one_column, 0)
        put(row).start()
        for step, chunk in plan[row]:
            step(chunk)
    for row in range(max(0, slab_rows - 2), slab_rows):
        put(row).wait()
    finish()


def owner_scratch(partial, row_devices):
    parts, slab_rows, modes, lanes = partial.shape
    owned = modes // row_devices
    chunks = min(4, slab_rows)
    return jax.ShapeDtypeStruct((row_devices, slab_rows, owned, lanes), wide), [
        pltpu.VMEM((2, slab_rows, modes, lanes), wide),
        pltpu.VMEM((slab_rows, modes, lanes), wide),
        pltpu.VMEM((slab_rows, modes, lanes), wide),
        pltpu.VMEM((row_devices, slab_rows, owned, lanes), wide),
    ], [
        pltpu.SemaphoreType.DMA((2, 2, chunks)),
        pltpu.SemaphoreType.DMA((2, chunks)),
        pltpu.SemaphoreType.DMA((2, chunks, row_devices - 1)),
    ]


vmem_spec = pl.BlockSpec(memory_space=pltpu.VMEM)


def to_owner(partial):
    shape, buffers, sems = owner_scratch(partial, lax.axis_size("gx"))
    planes = pl.pallas_call(
        to_owner_kernel,
        in_specs=[vmem_spec],
        out_specs=vmem_spec,
        out_shape=shape,
        scratch_shapes=buffers + sems,
        compiler_params=pltpu.CompilerParams(
            collective_id=0, has_side_effects=True, vmem_limit_bytes=VMEM_LIMIT
        ),
        name="to_owner",
    )(partial)
    return planes.reshape(-1, planes.shape[3])


def to_owner_masking(partial, cotangent, hash_key, channels, all_columns):
    shape, buffers, sems = owner_scratch(partial, lax.axis_size("gx"))
    _, cells, depth_cells = cotangent.shape
    planes, masked = pl.pallas_call(
        functools.partial(masking_kernel, all_columns, channels),
        in_specs=[
            pl.BlockSpec(memory_space=pltpu.SMEM),
            vmem_spec,
            pl.BlockSpec(memory_space=pl.ANY),
        ],
        out_specs=[vmem_spec, pl.BlockSpec(memory_space=pl.ANY)],
        out_shape=[shape, jax.ShapeDtypeStruct(cotangent.shape, low)],
        scratch_shapes=buffers
        + [
            pltpu.VMEM((2, cells, depth_cells), low),
            pltpu.VMEM((2, cells, depth_cells), low),
            pltpu.VMEM((channels, depth_cells), jnp.int32),
            pltpu.SemaphoreType.DMA((2,)),
            pltpu.SemaphoreType.DMA((2,)),
        ]
        + sems,
        compiler_params=pltpu.CompilerParams(
            collective_id=1, has_side_effects=True, vmem_limit_bytes=VMEM_LIMIT
        ),
        name="to_owner_masking",
    )(hash_key, partial, cotangent)
    return planes.reshape(-1, planes.shape[3]), masked


def from_owner_kernel(spread_ref, out_ref, peer_sem, across_sem, mate_sem):
    row, column, mate, across = neighbours()
    row_devices, slab_rows = spread_ref.shape[:2]
    chunks = peer_sem.shape[1]
    rows = slab_rows // chunks
    greet(row, column, mate, across)

    def window(chunk):
        return pl.ds(chunk * rows, rows)

    def peer_copy(chunk, offset):
        peer = lax.rem(row + offset, row_devices)
        return send(
            spread_ref.at[peer, window(chunk)],
            out_ref.at[column, row, window(chunk)],
            peer_sem,
            (chunk, offset - 1),
            (peer, column),
        )

    def part_copy(chunk, part, sem, at, target):
        view = out_ref.at[part, :, window(chunk)]
        return send(view, view, sem, at, (row, target))

    def across_copy(chunk):
        return part_copy(chunk, column, across_sem, (chunk,), across)

    def mate_copy(chunk, half):
        return part_copy(chunk, across if half else column, mate_sem, (half, chunk), mate)

    for chunk in range(chunks):

        def start_peer(offset, carry):
            peer_copy(chunk, offset).start()
            return carry

        lax.fori_loop(1, row_devices, start_peer, 0)
    out_ref[column, row] = spread_ref[row]
    for chunk in range(chunks):

        def wait_peer(offset, carry):
            peer_copy(chunk, offset).wait_recv()
            return carry

        lax.fori_loop(1, row_devices, wait_peer, 0)
        across_copy(chunk).start()
        mate_copy(chunk, 0).start()
    for chunk in range(chunks):
        across_copy(chunk).wait_recv()
        mate_copy(chunk, 1).start()
    for chunk in range(chunks):
        for half in range(2):
            mate_copy(chunk, half).wait()
        across_copy(chunk).wait_send()

        def wait_sent(offset, carry):
            peer_copy(chunk, offset).wait_send()
            return carry

        lax.fori_loop(1, row_devices, wait_sent, 0)


def from_owner(planes, kept):
    row_devices = lax.axis_size("gx")
    spread = planes.reshape(row_devices, -1, kept, planes.shape[1])
    slab_rows = spread.shape[1]
    chunks = min(4, slab_rows)
    return pl.pallas_call(
        from_owner_kernel,
        in_specs=[vmem_spec],
        out_specs=vmem_spec,
        out_shape=jax.ShapeDtypeStruct((lax.axis_size("gy"), *spread.shape), wide),
        scratch_shapes=[
            pltpu.SemaphoreType.DMA((2, chunks, row_devices - 1)),
            pltpu.SemaphoreType.DMA((2, chunks)),
            pltpu.SemaphoreType.DMA((2, 2, chunks)),
        ],
        compiler_params=pltpu.CompilerParams(
            collective_id=2, has_side_effects=True, vmem_limit_bytes=VMEM_LIMIT
        ),
        name="from_owner",
    )(spread)


def local(layer_input, cotangent, spectral_weight, bypass_weight, channel_bias, hash_key):
    slab_rows, slab_columns, channels, depth_cells = layer_input.shape
    row_devices = lax.axis_size("gx")
    column_devices = lax.axis_size("gy")
    owned_columns, owned_modes, kept_rows, pairs = spectral_weight.shape
    all_rows = slab_rows * row_devices
    all_columns = slab_columns * column_devices
    kept_columns = owned_columns * column_devices
    column_offset = lax.axis_index("gy") * slab_columns
    cells = slab_columns * channels

    one_channel = np.eye(channels)
    down = hartley_table(kept_columns, all_columns)
    down_all = low_pair(np.kron(down.T, one_channel))
    up_all = low_pair(
        np.kron(
            down.reshape(kept_columns, column_devices, slab_columns).transpose(1, 0, 2), one_channel
        )
    )
    down_wide, down_rest = (
        lax.dynamic_slice_in_dim(table, column_offset * channels, cells, 0) for table in down_all
    )
    up_wide, up_rest = (
        lax.dynamic_index_in_dim(table, lax.axis_index("gy"), 0, keepdims=False)
        for table in up_all
    )
    across = hartley_table(kept_rows, all_rows)
    one_mode = np.eye(owned_modes)
    across_wide = np.einsum("kx,mn->mkxn", across, one_mode).reshape(
        owned_modes * kept_rows, all_rows * owned_modes
    )
    back_wide, back_rest = low_pair(across_wide.T)
    across_wide, across_rest = low_pair(across_wide)
    pick_c = np.kron(one_channel, np.ones((1, channels)))
    pick_d = np.kron(np.ones((1, channels)), one_channel)
    sum_c, sum_d = low_constant(pick_c.T), low_constant(pick_d.T)
    pick_c, pick_d = low_constant(pick_c), low_constant(pick_d)
    depth_low, depth_rest = low_pair(depth_table())
    depth_stack = jnp.concatenate([depth_low, depth_low, depth_rest], axis=0)
    group = max(1, 256 // channels)
    one_group = jnp.eye(group, dtype=low)
    bypass_in = jnp.kron(one_group, bypass_weight.T)
    bypass_out = jnp.kron(one_group, bypass_weight)

    source = layer_input.reshape(slab_rows, cells, depth_cells)
    weight = spectral_weight.reshape(owned_columns, owned_modes * kept_rows, pairs)

    planes, masked = to_owner_masking(
        forward_local(source, depth_low, down_wide, down_rest, column_devices),
        cotangent.reshape(source.shape),
        hash_key,
        channels,
        all_columns,
    )
    input_modes, spread = mix_modes(
        planes, weight, across_wide, across_rest, back_wide, back_rest, pick_c, sum_d
    )
    dpre, partial, weight_local, sums_local = middle_pass(
        from_owner(spread, owned_modes),
        source,
        masked,
        up_wide,
        up_rest,
        depth_stack,
        depth_low,
        down_wide,
        bypass_in,
        channel_bias[:, None],
    )
    weight_local = jnp.einsum(
        "acad->cd", weight_local.reshape(group, channels, group, channels)
    )
    bias_local = jnp.sum(sums_local[0].reshape(slab_columns, channels), axis=0) / depth_low[
        0, 0
    ].astype(wide)
    weight_total, bias_total = lax.psum((weight_local, bias_local), ("gx", "gy"))
    norm_scale = 1.0 / math.sqrt(all_rows * all_columns * depth_cells)
    grad_spectral, spread_back = mix_back(
        to_owner(partial), input_modes, weight, across_wide, back_wide, pick_c, pick_d, sum_c
    )
    grad_input = last_pass(
        from_owner(spread_back, owned_modes), dpre, up_wide, depth_low, bypass_out
    )
    return (
        grad_input.reshape(layer_input.shape),
        grad_spectral.reshape(spectral_weight.shape),
        weight_total * norm_scale,
        bias_total * norm_scale,
    )


def solution(mesh):
    return jax.shard_map(
        local,
        mesh=mesh,
        in_specs=(
            P("gx", "gy", None, None),
            P("gx", "gy", None, None),
            P("gy", "gx", None, None),
            P(),
            P(),
            P(),
        ),
        out_specs=(P("gx", "gy", None, None), P("gy", "gx", None, None), P(), P()),
        check_vma=False,
    )
```

```python
import functools
import math

import jax
import jax.numpy as jnp
import ml_dtypes
import numpy as np
from jax import lax
from jax.experimental import pallas as pl
from jax.experimental.pallas import tpu as pltpu
from jax.sharding import PartitionSpec as P

LZ = 64
LT = 8
KZ = 16
KT = 4

keep_level = 6554
keep_scale = 1.0 / 0.9
gelu_cubic = 0.044715
mixer_one = -1640531535
mixer_two = -2048144789
mixer_three = -1028477387
low = jnp.bfloat16
wide = jnp.float32
VMEM_LIMIT = 56 * 1024 * 1024


def hartley_table(kept, length):
    wanted = np.arange(kept)
    frequency = np.where(wanted < kept // 2, wanted, wanted + (length - kept))
    residue = frequency[:, None] * np.arange(length)[None, :] % length
    radians = residue * (2.0 * math.pi / length)
    return (np.cos(radians) + np.sin(radians)) / math.sqrt(length)


def depth_table():
    depth_part = hartley_table(KZ, LZ)
    time_part = hartley_table(KT, LT)
    joined = depth_part[:, None, :, None] * time_part[None, :, None, :]
    return joined.reshape(KZ * KT, LZ * LT)


def low_constant(values):
    return jnp.asarray(np.asarray(values, np.float32).astype(ml_dtypes.bfloat16))


def low_pair(values):
    high = np.asarray(values, np.float32).astype(ml_dtypes.bfloat16)
    return jnp.asarray(high), low_constant(values - high.astype(np.float64))


def halves(values):
    high = values.astype(low)
    return high, (values - high.astype(wide)).astype(low)


def scramble(hashed):
    hashed = jnp.bitwise_xor(hashed, lax.shift_right_logical(hashed, jnp.int32(16)))
    hashed = hashed * jnp.int32(mixer_two)
    hashed = jnp.bitwise_xor(hashed, lax.shift_right_logical(hashed, jnp.int32(13)))
    hashed = hashed * jnp.int32(mixer_three)
    return jnp.bitwise_xor(hashed, lax.shift_right_logical(hashed, jnp.int32(16)))


def scaled_slope(preact):
    factor = math.sqrt(2.0 / math.pi)
    square = preact * preact
    tanh_value = jnp.tanh(preact * (square * (factor * gelu_cubic) + factor))
    inner = preact * (
        square * (0.5 * keep_scale * factor * 3.0 * gelu_cubic) + 0.5 * keep_scale * factor
    )
    return (1.0 + tanh_value) * (inner * (1.0 - tanh_value) + 0.5 * keep_scale)


def dot(a, b):
    return lax.dot_general(a, b, (((1,), (0,)), ((), ())), preferred_element_type=wide)


def dot_rows(a, b):
    return lax.dot_general(a, b, (((1,), (1,)), ((), ())), preferred_element_type=wide)


def dot_fine(a, b):
    return dot(a[0], b[0]) + (dot(a[1], b[0]) + dot(a[0], b[1]))


def forward_kernel(source_ref, depth_ref, down_ref, rest_ref, out_ref, swept, swept_rest):
    rows = source_ref.shape[0]
    modes = depth_ref.shape[0]
    lanes = out_ref.shape[3]
    for row in range(rows):
        window = slice(row * modes, (row + 1) * modes)
        swept[window, :], swept_rest[window, :] = halves(dot_rows(depth_ref[...], source_ref[row]))
    for part in range(out_ref.shape[0]):
        window = slice(part * lanes, (part + 1) * lanes)
        out_ref[part] = dot_fine(
            (swept[...], swept_rest[...]), (down_ref[:, window], rest_ref[:, window])
        ).reshape(rows, modes, lanes)


def forward_local(source, depth_low, down_wide, down_rest, parts):
    slab_rows, cells, depth_cells = source.shape
    modes = depth_low.shape[0]
    lanes = down_wide.shape[1] // parts
    step = min(4, slab_rows)
    return pl.pallas_call(
        forward_kernel,
        grid=(slab_rows // step,),
        in_specs=[
            pl.BlockSpec((step, cells, depth_cells), lambda i: (i, 0, 0)),
            pl.BlockSpec(depth_low.shape, lambda i: (0, 0)),
            pl.BlockSpec(down_wide.shape, lambda i: (0, 0)),
            pl.BlockSpec(down_rest.shape, lambda i: (0, 0)),
        ],
        out_specs=pl.BlockSpec((parts, step, modes, lanes), lambda i: (0, i, 0, 0)),
        out_shape=jax.ShapeDtypeStruct((parts, slab_rows, modes, lanes), wide),
        scratch_shapes=[pltpu.VMEM((step * modes, cells), low)] * 2,
        compiler_params=pltpu.CompilerParams(vmem_limit_bytes=VMEM_LIMIT),
        name="forward_local",
    )(source, depth_low, down_wide, down_rest)


def mix_kernel(
    planes_ref,
    weight_ref,
    across_ref,
    across_rest,
    back_ref,
    back_rest,
    pick_c,
    sum_d,
    modes_ref,
    out_ref,
    split,
    mixed,
):
    ky = pl.program_id(0)
    steps, _, channels = split.shape

    @pl.when(ky == 0)
    def _():
        modes = dot_fine((across_ref[...], across_rest[...]), halves(planes_ref[...]))
        modes_ref[...] = modes
        for part in range(steps):
            split[part] = modes[:, part * channels : (part + 1) * channels]

    high, rest = halves(split[ky])
    spread = dot(high, pick_c[...]) + dot(rest, pick_c[...])
    high, rest = halves(spread * weight_ref[0].astype(wide))
    mixed[ky] = dot(high, sum_d[...]) + dot(rest, sum_d[...])

    @pl.when(ky == steps - 1)
    def _():
        joined = jnp.concatenate([mixed[part] for part in range(steps)], axis=1)
        out_ref[...] = dot_fine((back_ref[...], back_rest[...]), halves(joined))


def mix_back_kernel(
    planes_ref,
    modes_ref,
    weight_ref,
    across_ref,
    back_ref,
    pick_c,
    pick_d,
    sum_c,
    grad_ref,
    out_ref,
    split_in,
    split,
    mixed,
):
    ky = pl.program_id(0)
    steps, _, channels = split.shape

    @pl.when(ky == 0)
    def _():
        modes = dot(across_ref[...], planes_ref[...].astype(low))
        for part in range(steps):
            window = slice(part * channels, (part + 1) * channels)
            split[part] = modes[:, window].astype(low)
            split_in[part] = modes_ref[:, window].astype(low)

    spread = dot(split[ky], pick_d[...])
    grad_ref[0] = dot(split_in[ky], pick_c[...]) * spread
    product = spread.astype(low) * weight_ref[0]
    mixed[ky] = dot(product, sum_c[...]).astype(low)

    @pl.when(ky == steps - 1)
    def _():
        joined = jnp.concatenate([mixed[part] for part in range(steps)], axis=1)
        out_ref[...] = dot(back_ref[...], joined)


def whole_spec(array):
    return pl.BlockSpec(array.shape, lambda i: (0,) * array.ndim)


def kept_spec(array):
    return pl.BlockSpec(
        array.shape, lambda i: (0,) * array.ndim, pipeline_mode=pl.Buffered(1)
    )


def mix_modes(planes, weight, across, across_rest, back, back_rest, pick_c, sum_d):
    kept_rows, lanes = across.shape[0], planes.shape[1]
    steps, _, pairs = weight.shape
    channels = lanes // steps
    return pl.pallas_call(
        mix_kernel,
        grid=(steps,),
        in_specs=[
            whole_spec(planes),
            pl.BlockSpec((1, kept_rows, pairs), lambda i: (i, 0, 0)),
            whole_spec(across),
            whole_spec(across_rest),
            whole_spec(back),
            whole_spec(back_rest),
            whole_spec(pick_c),
            whole_spec(sum_d),
        ],
        out_specs=[
            pl.BlockSpec((kept_rows, lanes), lambda i: (0, 0)),
            pl.BlockSpec(planes.shape, lambda i: (0, 0)),
        ],
        out_shape=[
            jax.ShapeDtypeStruct((kept_rows, lanes), wide),
            jax.ShapeDtypeStruct(planes.shape, wide),
        ],
        scratch_shapes=[
            pltpu.VMEM((steps, kept_rows, channels), wide),
            pltpu.VMEM((steps, kept_rows, channels), wide),
        ],
        compiler_params=pltpu.CompilerParams(vmem_limit_bytes=VMEM_LIMIT),
        name="mix_modes",
    )(planes, weight, across, across_rest, back, back_rest, pick_c, sum_d)


def mix_back(planes, modes, weight, across, back, pick_c, pick_d, sum_c):
    kept_rows, lanes = across.shape[0], planes.shape[1]
    steps, _, pairs = weight.shape
    channels = lanes // steps
    return pl.pallas_call(
        mix_back_kernel,
        grid=(steps,),
        in_specs=[
            whole_spec(planes),
            whole_spec(modes),
            pl.BlockSpec((1, kept_rows, pairs), lambda i: (i, 0, 0)),
            whole_spec(across),
            whole_spec(back),
            whole_spec(pick_c),
            whole_spec(pick_d),
            whole_spec(sum_c),
        ],
        out_specs=[
            pl.BlockSpec((1, kept_rows, pairs), lambda i: (i, 0, 0)),
            pl.BlockSpec(planes.shape, lambda i: (0, 0)),
        ],
        out_shape=[
            jax.ShapeDtypeStruct((steps, kept_rows, pairs), wide),
            jax.ShapeDtypeStruct(planes.shape, wide),
        ],
        scratch_shapes=[
            pltpu.VMEM((steps, kept_rows, channels), low),
            pltpu.VMEM((steps, kept_rows, channels), low),
            pltpu.VMEM((steps, kept_rows, channels), low),
        ],
        compiler_params=pltpu.CompilerParams(vmem_limit_bytes=VMEM_LIMIT),
        name="mix_back",
    )(planes, modes, weight, across, back, pick_c, pick_d, sum_c)


def joined_parts(gathered_ref):
    parts, devices, rows, owned, lanes = gathered_ref.shape
    return jnp.concatenate(
        [
            jnp.concatenate(
                [gathered_ref[part, :, row].reshape(devices * owned, lanes) for row in range(rows)],
                axis=0,
            )
            for part in range(parts)
        ],
        axis=1,
    )


def column_modes(gathered_ref, up_ref, turned):
    rows, _, modes = turned.shape
    columns = dot(joined_parts(gathered_ref).astype(low), up_ref[...])
    for row in range(rows):
        turned[row] = columns[row * modes : (row + 1) * modes, :].T.astype(low)


def column_modes_fine(gathered_ref, up_ref, up_rest, turned):
    rows, _, stacked = turned.shape
    modes = stacked // 3
    columns = dot_fine(halves(joined_parts(gathered_ref)), (up_ref[...], up_rest[...]))
    for row in range(rows):
        high, rest = halves(columns[row * modes : (row + 1) * modes, :].T)
        turned[row] = jnp.concatenate([high, rest, high], axis=1)


def middle_kernel(
    channels,
    gathered_ref,
    source_ref,
    cotangent_ref,
    up_ref,
    up_rest,
    depth_ref,
    depth_low_ref,
    down_ref,
    bypass_ref,
    bias_ref,
    dpre_ref,
    planes_ref,
    small_ref,
    turned,
    preact,
    swept,
    weight_ref,
    sums_ref,
    modes_ref,
    landed,
    mate_in,
    across_out,
    across_in,
    peer_out,
    small,
    peers_in,
    pair_sums,
    small_peer_sem,
    small_pair_sem,
    *sems,
):
    step = pl.program_id(0)
    rows, cells, depth_cells = source_ref.shape
    modes = depth_low_ref.shape[0]
    lanes = modes_ref.shape[3]
    block = bypass_ref.shape[0]
    columns = cells // channels

    chunks, start_sums, pair_sum, side_sum, finish = to_owner_steps(
        modes_ref, landed, mate_in, across_out, across_in, peer_out, sems
    )

    @pl.when(step == 0)
    def _():
        greet(*neighbours())
        weight_ref[...] = jnp.zeros_like(weight_ref)
        sums_ref[...] = jnp.zeros_like(sums_ref)

    column_modes_fine(gathered_ref, up_ref, up_rest, turned)
    for row in range(rows):
        for start in range(0, cells, block):
            window = slice(start, start + block)
            preact[window, :] = dot(turned[row, window, :], depth_ref[...]) + dot(
                bypass_ref[...], source_ref[row, window, :]
            )
        def one_column(column, carry):
            start = pl.multiple_of(column * channels, channels)
            window = pl.ds(start, channels)
            slope = scaled_slope(preact[window, :] + bias_ref[...])
            value = cotangent_ref[row, window, :].astype(wide) * slope
            dpre_ref[row, window, :] = value.astype(low)
            return carry

        lax.fori_loop(0, columns, one_column, 0, unroll=4)
        depth_sums = dot_rows(depth_low_ref[...], dpre_ref[row])
        sums_ref[...] += depth_sums[:8, :]
        swept[row * modes : (row + 1) * modes, :] = depth_sums.astype(low)
        total = weight_ref[...]
        for start in range(0, cells, block):
            window = slice(start, start + block)
            total += dot_rows(source_ref[row, window, :], dpre_ref[row, window, :])
        weight_ref[...] = total
    for part in range(modes_ref.shape[0]):
        modes_ref[part, pl.ds(step * rows, rows)] = dot(
            swept[...], down_ref[:, part * lanes : (part + 1) * lanes]
        ).reshape(rows, modes, lanes)
    for chunk in range(chunks):

        @pl.when(step == chunk)
        def _(chunk=chunk):
            start_sums(chunk)
            if chunk >= 1:
                pair_sum(chunk - 1)
            if chunk >= 2:
                side_sum(chunk - 2)

    @pl.when(step == chunks - 1)
    def _():
        row, column, mate, across = neighbours()
        row_devices = peers_in.shape[0]

        def peer_copy(offset):
            peer = lax.rem(row + offset, row_devices)
            return send(
                small, peers_in.at[row], small_peer_sem, (offset - 1,), (peer, column)
            )

        def pair_copy(which, target):
            return send(
                pair_sums.at[2 * which],
                pair_sums.at[2 * which + 1],
                small_pair_sem,
                (which,),
                (row, target),
            )

        small[...] = jnp.zeros_like(small)
        total = weight_ref[:channels, :channels]
        for at in range(channels, block, channels):
            total += weight_ref[at : at + channels, at : at + channels]
        small[:channels, :channels] = total
        total = sums_ref[:, :channels]
        for at in range(channels, cells, channels):
            total += sums_ref[:, at : at + channels]
        small[channels:, :channels] = total
        peers_in[row] = small[...]

        def start_peer(offset, carry):
            peer_copy(offset).start()
            return carry

        def wait_peer(offset, carry):
            peer_copy(offset).wait()
            return carry

        lax.fori_loop(1, row_devices, start_peer, 0)
        pair_sum(chunks - 1)
        if chunks >= 2:
            side_sum(chunks - 2)
        lax.fori_loop(1, row_devices, wait_peer, 0)
        total = peers_in[0]
        for peer in range(1, row_devices):
            total += peers_in[peer]
        pair_sums[0] = total
        pair_copy(0, mate).start()
        side_sum(chunks - 1)
        pair_copy(0, mate).wait()
        pair_sums[2] = pair_sums[0] + pair_sums[1]
        pair_copy(1, across).start()
        finish()
        planes_ref[...] = landed[...]
        pair_copy(1, across).wait()
        small_ref[...] = pair_sums[2] + pair_sums[3]


def middle_pass(
    gathered, source, cotangent, up, up_rest, depth, depth_low, down, bypass, bias
):
    parts, devices, slab_rows, owned, lanes = gathered.shape
    modes = devices * owned
    _, cells, depth_cells = source.shape
    channels = bias.shape[0]
    block = bypass.shape[0]
    step = min(4, slab_rows)
    row_spec = pl.BlockSpec((step, cells, depth_cells), lambda i: (i, 0, 0))
    partial = jax.ShapeDtypeStruct((parts, slab_rows, modes, lanes), wide)
    planes, buffers, sems = owner_scratch(partial, devices, slab_rows // step)
    small = (channels + 8, 128)
    return pl.pallas_call(
        functools.partial(middle_kernel, channels),
        grid=(slab_rows // step,),
        in_specs=[
            pl.BlockSpec((parts, devices, step, owned, lanes), lambda i: (0, 0, i, 0, 0)),
            row_spec,
            row_spec,
            kept_spec(up),
            kept_spec(up_rest),
            kept_spec(depth),
            kept_spec(depth_low),
            kept_spec(down),
            kept_spec(bypass),
            kept_spec(bias),
        ],
        out_specs=[
            row_spec,
            pl.BlockSpec(planes.shape, lambda i: (0, 0, 0, 0)),
            pl.BlockSpec(small, lambda i: (0, 0)),
        ],
        out_shape=[
            jax.ShapeDtypeStruct(source.shape, low),
            planes,
            jax.ShapeDtypeStruct(small, wide),
        ],
        scratch_shapes=[
            pltpu.VMEM((step, cells, 3 * modes), low),
            pltpu.VMEM((cells, depth_cells), wide),
            pltpu.VMEM((step * modes, cells), low),
            pltpu.VMEM((block, block), wide),
            pltpu.VMEM((8, cells), wide),
            pltpu.VMEM(partial.shape, wide),
            pltpu.VMEM(planes.shape, wide),
            *buffers,
            pltpu.VMEM(small, wide),
            pltpu.VMEM((devices, *small), wide),
            pltpu.VMEM((4, *small), wide),
            pltpu.SemaphoreType.DMA((2, devices - 1)),
            pltpu.SemaphoreType.DMA((2, 2)),
            *sems,
        ],
        compiler_params=pltpu.CompilerParams(
            collective_id=0, has_side_effects=True, vmem_limit_bytes=VMEM_LIMIT
        ),
        name="middle_pass",
    )(gathered, source, cotangent, up, up_rest, depth, depth_low, down, bypass, bias)


def last_kernel(gathered_ref, dpre_ref, up_ref, depth_ref, bypass_ref, out_ref, turned):
    rows, cells, _ = dpre_ref.shape
    block = bypass_ref.shape[0]
    column_modes(gathered_ref, up_ref, turned)
    for row in range(rows):
        for start in range(0, cells, block):
            window = slice(start, start + block)
            out_ref[row, window, :] = (
                dot(turned[row, window, :], depth_ref[...])
                + dot(bypass_ref[...], dpre_ref[row, window, :])
            ).astype(low)


def last_pass(gathered, dpre, up, depth, bypass):
    parts, devices, slab_rows, owned, lanes = gathered.shape
    modes = devices * owned
    _, cells, depth_cells = dpre.shape
    step = min(4, slab_rows)
    row_spec = pl.BlockSpec((step, cells, depth_cells), lambda i: (i, 0, 0))
    return pl.pallas_call(
        last_kernel,
        grid=(slab_rows // step,),
        in_specs=[
            pl.BlockSpec((parts, devices, step, owned, lanes), lambda i: (0, 0, i, 0, 0)),
            row_spec,
            whole_spec(up),
            whole_spec(depth),
            whole_spec(bypass),
        ],
        out_specs=row_spec,
        out_shape=jax.ShapeDtypeStruct(dpre.shape, low),
        scratch_shapes=[pltpu.VMEM((step, cells, modes), low)],
        compiler_params=pltpu.CompilerParams(vmem_limit_bytes=VMEM_LIMIT),
        name="last_pass",
    )(gathered, dpre, up, depth, bypass)


MESH = pl.DeviceIdType.MESH


def neighbours():
    row, column = lax.axis_index("gx"), lax.axis_index("gy")
    core, side = column % 2, column // 2
    return row, column, side * 2 + 1 - core, (1 - side) * 2 + core


def greet(row, column, mate, across):
    row_devices = lax.axis_size("gx")
    barrier = pltpu.get_barrier_semaphore()
    for target in (mate, across):
        pl.semaphore_signal(barrier, inc=1, device_id=(row, target), device_id_type=MESH)

    def signal_peer(offset, carry):
        pl.semaphore_signal(
            barrier,
            inc=1,
            device_id=(lax.rem(row + offset, row_devices), column),
            device_id_type=MESH,
        )
        return carry

    lax.fori_loop(1, row_devices, signal_peer, 0)
    pl.semaphore_wait(barrier, row_devices + 1)


def send(source, target, semaphores, at, device):
    return pltpu.make_async_remote_copy(
        src_ref=source,
        dst_ref=target,
        send_sem=semaphores.at[(0, *at)],
        recv_sem=semaphores.at[(1, *at)],
        device_id=device,
        device_id_type=MESH,
    )


def to_owner_steps(partial_ref, out_ref, mate_in, across_out, across_in, peer_out, sems):
    mate_sem, across_sem, peer_sem = sems
    _, slab_rows, _, _ = partial_ref.shape
    row, column, mate, across = neighbours()
    core, side = column % 2, column // 2
    row_devices, owned = peer_out.shape[0], peer_out.shape[2]
    chunks = mate_sem.shape[2]
    rows = slab_rows // chunks

    def window(chunk):
        return pl.ds(chunk * rows, rows)

    def mate_copy(chunk, half):
        return send(
            partial_ref.at[half * 2 + 1 - core, window(chunk)],
            mate_in.at[half, window(chunk)],
            mate_sem,
            (half, chunk),
            (row, mate),
        )

    def across_copy(chunk):
        return send(
            across_out.at[window(chunk)],
            across_in.at[window(chunk)],
            across_sem,
            (chunk,),
            (row, across),
        )

    def peer_copy(chunk, offset):
        peer = lax.rem(row + offset, row_devices)
        return send(
            peer_out.at[peer, window(chunk)],
            out_ref.at[row, window(chunk)],
            peer_sem,
            (chunk, offset - 1),
            (peer, column),
        )

    def start(chunk):
        for half in range(2):
            mate_copy(chunk, half).start()

    def pair_sum(chunk):
        for half in range(2):
            mate_copy(chunk, half).wait_recv()
        across_out[window(chunk)] = (
            partial_ref[across, window(chunk)] + mate_in[1 - side, window(chunk)]
        )
        across_copy(chunk).start()

    def side_sum(chunk):
        across_copy(chunk).wait_recv()
        total = (
            partial_ref[column, window(chunk)] + mate_in[side, window(chunk)]
        ) + across_in[window(chunk)]
        for peer in range(row_devices):
            peer_out[peer, window(chunk)] = total[:, peer * owned : (peer + 1) * owned, :]

        def start_peer(offset, carry):
            peer_copy(chunk, offset).start()
            return carry

        lax.fori_loop(1, row_devices, start_peer, 0)
        out_ref[row, window(chunk)] = peer_out[row, window(chunk)]

    def finish():
        for chunk in range(chunks):

            def wait_peer(offset, carry):
                copy = peer_copy(chunk, offset)
                copy.wait_recv()
                copy.wait_send()
                return carry

            lax.fori_loop(1, row_devices, wait_peer, 0)
            across_copy(chunk).wait_send()
            for half in range(2):
                mate_copy(chunk, half).wait_send()

    return chunks, start, pair_sum, side_sum, finish


def masking_kernel(
    all_columns,
    channels,
    key_ref,
    partial_ref,
    cotangent_ref,
    out_ref,
    masked_ref,
    mate_in,
    across_out,
    across_in,
    peer_out,
    held,
    made,
    offsets,
    in_sem,
    out_sem,
    *sems,
):
    slab_rows, cells, depth_cells = cotangent_ref.shape
    columns = cells // channels

    def fetch(row):
        return pltpu.make_async_copy(
            cotangent_ref.at[row], held.at[row % 2], in_sem.at[row % 2]
        )

    def put(row):
        return pltpu.make_async_copy(made.at[row % 2], masked_ref.at[row], out_sem.at[row % 2])

    fetch(0).start()
    offsets[...] = (
        lax.broadcasted_iota(jnp.int32, offsets.shape, 0) * depth_cells
        + lax.broadcasted_iota(jnp.int32, offsets.shape, 1)
    ) * jnp.int32(mixer_one)
    greet(*neighbours())
    chunks, start, pair_sum, side_sum, finish = to_owner_steps(
        partial_ref, out_ref, mate_in, across_out, across_in, peer_out, sems
    )
    for chunk in range(chunks):
        start(chunk)
    plan = {row: [] for row in range(slab_rows)}
    for chunk in range(chunks):
        plan[min(chunk, slab_rows - 1)].append((pair_sum, chunk))
    for chunk in range(chunks):
        plan[min(slab_rows - 1, (chunk + 1) * slab_rows // chunks)].append((side_sum, chunk))
    row_base = lax.axis_index("gx") * slab_rows
    column_base = lax.axis_index("gy") * columns
    stride = (channels * depth_cells * mixer_one + 2**31) % 2**32 - 2**31
    for row in range(slab_rows):
        if row + 1 < slab_rows:
            fetch(row + 1).start()
        fetch(row).wait()
        if row >= 2:
            put(row - 2).wait()
        first = ((row_base + row) * all_columns + column_base) * jnp.int32(stride) + key_ref[0]

        def one_column(column, carry):
            window = pl.ds(pl.multiple_of(column * channels, channels), channels)
            hashed = scramble(offsets[...] + (first + column * jnp.int32(stride)))
            hashed = scramble(jnp.bitwise_xor(hashed, key_ref[1]))
            keep = jnp.bitwise_and(hashed, jnp.int32(65535)) >= keep_level
            made[row % 2, window, :] = jnp.where(
                keep, held[row % 2, window, :].astype(wide), 0.0
            ).astype(low)
            return carry

        lax.fori_loop(0, columns, one_column, 0, unroll=4)
        put(row).start()
        for step, chunk in plan[row]:
            step(chunk)
    for row in range(max(0, slab_rows - 2), slab_rows):
        put(row).wait()
    finish()


def owner_scratch(partial, row_devices, chunks):
    parts, slab_rows, modes, lanes = partial.shape
    owned = modes // row_devices
    return jax.ShapeDtypeStruct((row_devices, slab_rows, owned, lanes), wide), [
        pltpu.VMEM((2, slab_rows, modes, lanes), wide),
        pltpu.VMEM((slab_rows, modes, lanes), wide),
        pltpu.VMEM((slab_rows, modes, lanes), wide),
        pltpu.VMEM((row_devices, slab_rows, owned, lanes), wide),
    ], [
        pltpu.SemaphoreType.DMA((2, 2, chunks)),
        pltpu.SemaphoreType.DMA((2, chunks)),
        pltpu.SemaphoreType.DMA((2, chunks, row_devices - 1)),
    ]


vmem_spec = pl.BlockSpec(memory_space=pltpu.VMEM)


def to_owner_masking(partial, cotangent, hash_key, channels, all_columns):
    shape, buffers, sems = owner_scratch(partial, lax.axis_size("gx"), min(4, partial.shape[1]))
    _, cells, depth_cells = cotangent.shape
    planes, masked = pl.pallas_call(
        functools.partial(masking_kernel, all_columns, channels),
        in_specs=[
            pl.BlockSpec(memory_space=pltpu.SMEM),
            vmem_spec,
            pl.BlockSpec(memory_space=pl.ANY),
        ],
        out_specs=[vmem_spec, pl.BlockSpec(memory_space=pl.ANY)],
        out_shape=[shape, jax.ShapeDtypeStruct(cotangent.shape, low)],
        scratch_shapes=buffers
        + [
            pltpu.VMEM((2, cells, depth_cells), low),
            pltpu.VMEM((2, cells, depth_cells), low),
            pltpu.VMEM((channels, depth_cells), jnp.int32),
            pltpu.SemaphoreType.DMA((2,)),
            pltpu.SemaphoreType.DMA((2,)),
        ]
        + sems,
        compiler_params=pltpu.CompilerParams(
            collective_id=1, has_side_effects=True, vmem_limit_bytes=VMEM_LIMIT
        ),
        name="to_owner_masking",
    )(hash_key, partial, cotangent)
    return planes.reshape(-1, planes.shape[3]), masked


def from_owner_kernel(spread_ref, out_ref, peer_sem, across_sem, mate_sem):
    row, column, mate, across = neighbours()
    row_devices, slab_rows = spread_ref.shape[:2]
    chunks = peer_sem.shape[1]
    rows = slab_rows // chunks
    greet(row, column, mate, across)

    def window(chunk):
        return pl.ds(chunk * rows, rows)

    def peer_copy(chunk, offset):
        peer = lax.rem(row + offset, row_devices)
        return send(
            spread_ref.at[peer, window(chunk)],
            out_ref.at[column, row, window(chunk)],
            peer_sem,
            (chunk, offset - 1),
            (peer, column),
        )

    def part_copy(chunk, part, sem, at, target):
        view = out_ref.at[part, :, window(chunk)]
        return send(view, view, sem, at, (row, target))

    def across_copy(chunk):
        return part_copy(chunk, column, across_sem, (chunk,), across)

    def mate_copy(chunk, half):
        return part_copy(chunk, across if half else column, mate_sem, (half, chunk), mate)

    for chunk in range(chunks):

        def start_peer(offset, carry):
            peer_copy(chunk, offset).start()
            return carry

        lax.fori_loop(1, row_devices, start_peer, 0)
    out_ref[column, row] = spread_ref[row]
    for chunk in range(chunks):

        def wait_peer(offset, carry):
            peer_copy(chunk, offset).wait_recv()
            return carry

        lax.fori_loop(1, row_devices, wait_peer, 0)
        across_copy(chunk).start()
        mate_copy(chunk, 0).start()
    for chunk in range(chunks):
        across_copy(chunk).wait_recv()
        mate_copy(chunk, 1).start()
    for chunk in range(chunks):
        for half in range(2):
            mate_copy(chunk, half).wait()
        across_copy(chunk).wait_send()

        def wait_sent(offset, carry):
            peer_copy(chunk, offset).wait_send()
            return carry

        lax.fori_loop(1, row_devices, wait_sent, 0)


def from_owner(planes, kept):
    row_devices = lax.axis_size("gx")
    spread = planes.reshape(row_devices, -1, kept, planes.shape[1])
    slab_rows = spread.shape[1]
    chunks = min(4, slab_rows)
    return pl.pallas_call(
        from_owner_kernel,
        in_specs=[vmem_spec],
        out_specs=vmem_spec,
        out_shape=jax.ShapeDtypeStruct((lax.axis_size("gy"), *spread.shape), wide),
        scratch_shapes=[
            pltpu.SemaphoreType.DMA((2, chunks, row_devices - 1)),
            pltpu.SemaphoreType.DMA((2, chunks)),
            pltpu.SemaphoreType.DMA((2, 2, chunks)),
        ],
        compiler_params=pltpu.CompilerParams(
            collective_id=2, has_side_effects=True, vmem_limit_bytes=VMEM_LIMIT
        ),
        name="from_owner",
    )(spread)


def local(layer_input, cotangent, spectral_weight, bypass_weight, channel_bias, hash_key):
    slab_rows, slab_columns, channels, depth_cells = layer_input.shape
    row_devices = lax.axis_size("gx")
    column_devices = lax.axis_size("gy")
    owned_columns, owned_modes, kept_rows, pairs = spectral_weight.shape
    all_rows = slab_rows * row_devices
    all_columns = slab_columns * column_devices
    kept_columns = owned_columns * column_devices
    column_offset = lax.axis_index("gy") * slab_columns
    cells = slab_columns * channels

    one_channel = np.eye(channels)
    down = hartley_table(kept_columns, all_columns)
    down_all = low_pair(np.kron(down.T, one_channel))
    up_all = low_pair(
        np.kron(
            down.reshape(kept_columns, column_devices, slab_columns).transpose(1, 0, 2), one_channel
        )
    )
    down_wide, down_rest = (
        lax.dynamic_slice_in_dim(table, column_offset * channels, cells, 0) for table in down_all
    )
    up_wide, up_rest = (
        lax.dynamic_index_in_dim(table, lax.axis_index("gy"), 0, keepdims=False)
        for table in up_all
    )
    across = hartley_table(kept_rows, all_rows)
    one_mode = np.eye(owned_modes)
    across_wide = np.einsum("kx,mn->mkxn", across, one_mode).reshape(
        owned_modes * kept_rows, all_rows * owned_modes
    )
    back_wide, back_rest = low_pair(across_wide.T)
    across_wide, across_rest = low_pair(across_wide)
    pick_c = np.kron(one_channel, np.ones((1, channels)))
    pick_d = np.kron(np.ones((1, channels)), one_channel)
    sum_c, sum_d = low_constant(pick_c.T), low_constant(pick_d.T)
    pick_c, pick_d = low_constant(pick_c), low_constant(pick_d)
    depth_low, depth_rest = low_pair(depth_table())
    depth_stack = jnp.concatenate([depth_low, depth_low, depth_rest], axis=0)
    group = max(1, 256 // channels)
    one_group = jnp.eye(group, dtype=low)
    bypass_in = jnp.kron(one_group, bypass_weight.T)
    bypass_out = jnp.kron(one_group, bypass_weight)

    source = layer_input.reshape(slab_rows, cells, depth_cells)
    weight = spectral_weight.reshape(owned_columns, owned_modes * kept_rows, pairs)

    planes, masked = to_owner_masking(
        forward_local(source, depth_low, down_wide, down_rest, column_devices),
        cotangent.reshape(source.shape),
        hash_key,
        channels,
        all_columns,
    )
    input_modes, spread = mix_modes(
        planes, weight, across_wide, across_rest, back_wide, back_rest, pick_c, sum_d
    )
    dpre, back_planes, small = middle_pass(
        from_owner(spread, owned_modes),
        source,
        masked,
        up_wide,
        up_rest,
        depth_stack,
        depth_low,
        down_wide,
        bypass_in,
        channel_bias[:, None],
    )
    weight_total = small[:channels, :channels]
    bias_total = small[channels, :channels] / depth_low[0, 0].astype(wide)
    norm_scale = 1.0 / math.sqrt(all_rows * all_columns * depth_cells)
    grad_spectral, spread_back = mix_back(
        back_planes.reshape(planes.shape),
        input_modes,
        weight,
        across_wide,
        back_wide,
        pick_c,
        pick_d,
        sum_c,
    )
    grad_input = last_pass(
        from_owner(spread_back, owned_modes), dpre, up_wide, depth_low, bypass_out
    )
    return (
        grad_input.reshape(layer_input.shape),
        grad_spectral.reshape(spectral_weight.shape),
        weight_total * norm_scale,
        bias_total * norm_scale,
    )


def solution(mesh):
    return jax.shard_map(
        local,
        mesh=mesh,
        in_specs=(
            P("gx", "gy", None, None),
            P("gx", "gy", None, None),
            P("gy", "gx", None, None),
            P(),
            P(),
            P(),
        ),
        out_specs=(P("gx", "gy", None, None), P("gy", "gx", None, None), P(), P()),
        check_vma=False,
    )
```
